128 devices in a mesh: rep: 16 (over z_lo, y, core), fsdp: 8 (over z_hi, x).
Axes of the slice: x: 4, y: 4, z: 4 (z_hi: 2, z_lo: 2; z = z_hi * 2 + z_lo), core: 2. Of those that a mesh axis runs over, the one named last changes fastest.
Arguments:
- tokens: bfloat16 [16, 2048, 8192], P('rep', 'fsdp'), may hold values from -6 to 6
- targets: bfloat16 [16, 2048, 512], P('rep', 'fsdp'), may hold values from -6 to 6
- block_master: float32 [16, 8192, 512], P('rep', 'fsdp'), may hold values from -0.0625 to 0.0625
- block_first: float32 [16, 8192, 512], P('rep', 'fsdp'), may hold values from -0.2 to 0.2
- block_second: float32 [16, 8192, 512], P('rep', 'fsdp'), may hold values from 0.0003 to 0.003
- frag_outer: float32 [8192, 512], P('fsdp'), may hold values from -6 to 6
- frag_inner: bfloat16 [16, 8192, 512], P('rep', 'fsdp'), may hold values from -6 to 6
- frag_momentum: float32 [8192, 512], P('fsdp'), may hold values from -6 to 6
Outputs:
- block_shift: float32 [16, 8192, 512], P('rep', 'fsdp')
- frag_params: float32 [8192, 512], P('fsdp')
- momentum_out: float32 [8192, 512], P('fsdp')
The draws below stay inside these ranges and needn't reach their ends.
All inputs are finite; a program needn't handle non-finite values.
Results may differ from the reference program's by a relative error of at most 0.0012.
Values may be sent and summed in bfloat16 or wider, within the bound.
No kernel may reach another device: no remote copies, remote signals or barrier semaphores. Data moves between devices by JAX's collectives and lax.ppermute only.
A program may use at most 128 MiB of HBM per device.

```python
import math
import jax
import jax.numpy as jnp
from jax import lax

D = 8192
KVW = 512
FW = 512
TOKENS_REP = 2048
N_REP = 16


def levels(own_key, shape, shards, smallest, high):
    def one(position, shards_of):
        heights = jax.random.uniform(jax.random.fold_in(jax.random.fold_in(own_key, 6), position), (shards_of,), jnp.float32, smallest / len(shards), high / len(shards))
        return jnp.repeat(jnp.exp(heights), shape[position] // shards_of).reshape((-1,) + (1,) * (len(shape) - position - 1))

    loudness = one(*shards[0])
    for cut in shards[1:]:
        loudness = loudness * one(*cut)
    return loudness


def bell_draw(stream_key, shape, width, reach, split=(), kind=jnp.bfloat16):
    values = width * jax.random.normal(stream_key, shape, jnp.float32)
    if split:
        values = values * levels(stream_key, shape, split, -0.22, 0.18)
    return jnp.clip(values, -reach, reach).astype(kind)


def setup_inputs(seed: int = 0) -> dict:
    arg_keys = jax.random.split(jax.random.key(seed), 9)
    tokens = bell_draw(arg_keys[0], (N_REP, TOKENS_REP, D), 1.0, 6.0, ((0, 16), (1, 8)))
    targets = bell_draw(arg_keys[1], (N_REP, TOKENS_REP, KVW), 1.0, 6.0, ((0, 16), (1, 8)))
    block_master = bell_draw(arg_keys[2], (N_REP, D, KVW), D ** -0.5, 0.0625, ((0, 16), (1, 8)), jnp.float32)
    block_first = bell_draw(arg_keys[3], (N_REP, D, KVW), 0.03, 0.2, ((0, 16), (1, 8)), jnp.float32)
    block_second = jnp.clip(jnp.exp(math.log(0.003) - 2.3025851 * jax.random.uniform(arg_keys[4], (N_REP, D, KVW), jnp.float32) ** levels(arg_keys[4], (N_REP, D, KVW), ((0, 16), (1, 8)), -0.2, 0.2)), 0.0003, 0.003)
    frag_outer = bell_draw(arg_keys[5], (D, FW), 1.0, 6.0, ((0, 8),), jnp.float32)
    frag_inner = bell_draw(arg_keys[6], (N_REP, D, FW), 1.0, 6.0, ((0, 16), (1, 8)))
    frag_momentum = bell_draw(arg_keys[7], (D, FW), 1.0, 6.0, ((0, 8),), jnp.float32)
    return dict(tokens=tokens, targets=targets, block_master=block_master, block_first=block_first, block_second=block_second, frag_outer=frag_outer, frag_inner=frag_inner, frag_momentum=frag_momentum)


def adam_update(weights, first, second, grad):
    first = 0.9 * first + 0.1 * grad
    second = 0.95 * second + 0.05 * grad * grad
    update = first / (jnp.sqrt(second) + 1e-08) + 0.1 * weights
    return (weights - 0.001 * update, first, second, update)

def replica_window(items):
    inputs, teacher, weights, first, second = items
    total = jnp.zeros_like(weights)
    for step in range(2):
        outputs = jnp.dot(inputs, weights.astype(jnp.bfloat16), preferred_element_type=jnp.float32)
        resid = (outputs - teacher.astype(jnp.float32)).astype(jnp.bfloat16)
        grad = lax.dot_general(inputs, resid, (((0,), (0,)), ((), ())), preferred_element_type=jnp.float32) / TOKENS_REP
        weights, first, second, update = adam_update(weights, first, second, grad)
        total = total + update
    return total

def reference(tokens, targets, block_master, block_first, block_second, frag_outer, frag_inner, frag_momentum):
    block_shift = lax.map(replica_window, (tokens, targets, block_master, block_first, block_second))
    delta = lax.optimization_barrier(jnp.sum(frag_outer[None] - frag_inner.astype(jnp.float32), axis=0)) / N_REP
    momentum_out = 0.9 * frag_momentum + delta
    frag_params = frag_outer - 0.7 * (0.9 * momentum_out + delta)
    return (block_shift, frag_params, momentum_out)
```

```python
import jax
import jax.numpy as jnp
from jax import lax
from jax.sharding import PartitionSpec as P


def adam_update(weights, first, second, grad):
    first = 0.9 * first + 0.1 * grad
    second = 0.95 * second + 0.05 * grad * grad
    update = first / (jnp.sqrt(second) + 1e-08) + 0.1 * weights
    return (weights - 0.001 * update, first, second, update)


def outer_nesterov(outer, momentum, delta):
    momentum_new = 0.9 * momentum + delta
    return (outer - 0.7 * (0.9 * momentum_new + delta), momentum_new)


def shards(
    tokens, targets, block_master, block_first, block_second, frag_outer, frag_inner, frag_momentum
):
    inputs = tokens[0]
    teacher = targets[0].astype(jnp.float32)
    weights = block_master[0]
    first = block_first[0]
    second = block_second[0]
    groups = lax.axis_size("fsdp")
    replicas = lax.axis_size("rep")
    tok_local, features = inputs.shape
    tok_all = tok_local * groups
    rows, width = weights.shape
    blocks = inputs.reshape(tok_local, groups, rows).transpose(1, 0, 2)
    columns = lax.all_to_all(blocks, "fsdp", 0, 0).reshape(tok_all, rows)
    frag_rows = frag_inner.shape[1] // replicas
    pieces = lax.all_to_all(
        frag_inner[0].reshape(replicas, frag_rows, -1), "rep", 0, 0
    )
    piece_sum = jnp.sum(pieces.astype(jnp.float32), axis=0)
    inner_sum = lax.all_gather(piece_sum, "rep", axis=0, tiled=True)
    total = jnp.zeros_like(weights)
    for step in range(2):
        compute_w = weights.astype(jnp.bfloat16)
        partial_out = jnp.dot(columns, compute_w, preferred_element_type=jnp.float32)
        sent = partial_out.astype(jnp.bfloat16).reshape(groups, tok_local, width)
        arrived = lax.all_to_all(sent, "fsdp", 0, 0)
        outputs = jnp.sum(arrived.astype(jnp.float32), axis=0)
        resid_local = (outputs - teacher).astype(jnp.bfloat16)
        resid = lax.all_to_all(
            jnp.broadcast_to(resid_local[None], (groups, tok_local, width)), "fsdp", 0, 0
        ).reshape(tok_all, width)
        grad = (
            lax.dot_general(
                columns, resid, (((0,), (0,)), ((), ())), preferred_element_type=jnp.float32
            )
            / tok_all
        )
        weights, first, second, update = adam_update(weights, first, second, grad)
        total = total + update
    delta = frag_outer - inner_sum / replicas
    frag_params, momentum_out = outer_nesterov(frag_outer, frag_momentum, delta)
    return (total[None], frag_params, momentum_out)


def solution(mesh):
    in_specs = (
        P("rep", "fsdp", None),
        P("rep", "fsdp", None),
        P("rep", "fsdp", None),
        P("rep", "fsdp", None),
        P("rep", "fsdp", None),
        P("fsdp", None),
        P("rep", "fsdp", None),
        P("fsdp", None),
    )
    out_specs = (P("rep", "fsdp", None), P("fsdp", None), P("fsdp", None))
    return jax.shard_map(shards, mesh=mesh, in_specs=in_specs, out_specs=out_specs, check_vma=False)
```

```python
import jax
import jax.numpy as jnp
from jax import lax
from jax.sharding import PartitionSpec as P

NZ, NX = 2, 4


def adam_update(weights, first, second, grad):
    first = 0.9 * first + 0.1 * grad
    second = 0.95 * second + 0.05 * grad * grad
    update = first / (jnp.sqrt(second) + 1e-08) + 0.1 * weights
    return (weights - 0.001 * update, first, second, update)


def outer_nesterov(outer, momentum, delta):
    momentum_new = 0.9 * momentum + delta
    return (outer - 0.7 * (0.9 * momentum_new + delta), momentum_new)


def shift(value, dz, dx):
    pairs = [
        (z * NX + x, (z + dz) % NZ * NX + (x + dx) % NX) for z in range(NZ) for x in range(NX)
    ]
    return lax.ppermute(value, "fsdp", pairs)


def f32(value):
    return value.astype(jnp.float32)


def bf16(value):
    return value.astype(jnp.bfloat16)


def sum_x_first(part, teacher):
    arrived = [shift(bf16(part[:, dx]), 0, -dx) for dx in range(1, NX)]
    own = part[:, 0] + sum(f32(a) for a in arrived)
    other = f32(shift(bf16(own), 1, 0))
    outputs = jnp.stack([own[0] + other[1], own[1] + other[0]])
    resid = bf16(outputs - teacher)
    return jnp.stack([resid] + [shift(resid, 0, dx) for dx in range(1, NX)], axis=1)


def sum_z_first(part, teacher):
    own = part[0] + f32(shift(bf16(part[1]), 1, 0))
    arrived = [shift(bf16(own[dx]), 0, -dx) for dx in range(1, NX)]
    resid = bf16(own[0] + sum(f32(a) for a in arrived) - teacher[0])
    row = jnp.stack([resid] + [shift(resid, 0, dx) for dx in range(1, NX)])
    return jnp.stack([row, shift(row, 1, 0)])


def shards(
    tokens, targets, block_master, block_first, block_second, frag_outer, frag_inner, frag_momentum
):
    inputs = tokens[0]
    groups = lax.axis_size("fsdp")
    replicas = lax.axis_size("rep")
    tok_local, features = inputs.shape
    tok_all = tok_local * groups
    rows, width = block_master.shape[1:]
    me = lax.axis_index("fsdp")
    my_z, my_x = me // NX, me % NX
    blocks = []
    for dz in range(NZ):
        for dx in range(NX):
            owner = (my_z + dz) % NZ * NX + (my_x + dx) % NX
            piece = lax.dynamic_slice_in_dim(inputs, owner * rows, rows, axis=1)
            blocks.append(piece if (dz, dx) == (0, 0) else shift(piece, dz, dx))
    columns = jnp.concatenate(blocks, axis=0)
    teacher = f32(jnp.stack([targets[0], shift(targets[0], 1, 0)]))

    frag_rows = frag_inner.shape[1] // replicas
    pieces = lax.all_to_all(
        frag_inner[0].reshape(replicas, frag_rows, -1), "rep", 0, 0
    )
    piece_sum = jnp.sum(f32(pieces), axis=0)
    inner_sum = lax.all_gather(piece_sum, "rep", axis=0, tiled=True)

    half = width // 2
    shifts = []
    for cut, sum_outputs in ((0, sum_x_first), (half, sum_z_first)):
        span = slice(cut, cut + half)
        weights, first, second = (
            a[0, :, span] for a in (block_master, block_first, block_second)
        )
        total = jnp.zeros_like(weights)
        for step in range(2):
            part = jnp.dot(columns, bf16(weights), preferred_element_type=jnp.float32)
            resid = sum_outputs(part.reshape(NZ, NX, tok_local, half), teacher[:, :, span])
            grad = (
                lax.dot_general(
                    columns,
                    resid.reshape(tok_all, half),
                    (((0,), (0,)), ((), ())),
                    preferred_element_type=jnp.float32,
                )
                / tok_all
            )
            weights, first, second, update = adam_update(weights, first, second, grad)
            total = total + update
        shifts.append(total)
    block_shift = jnp.concatenate(shifts, axis=1)
    delta = frag_outer - inner_sum / replicas
    frag_params, momentum_out = outer_nesterov(frag_outer, frag_momentum, delta)
    return (block_shift[None], frag_params, momentum_out)


def solution(mesh):
    in_specs = (
        P("rep", "fsdp", None),
        P("rep", "fsdp", None),
        P("rep", "fsdp", None),
        P("rep", "fsdp", None),
        P("rep", "fsdp", None),
        P("fsdp", None),
        P("rep", "fsdp", None),
        P("fsdp", None),
    )
    out_specs = (P("rep", "fsdp", None), P("fsdp", None), P("fsdp", None))
    return jax.shard_map(shards, mesh=mesh, in_specs=in_specs, out_specs=out_specs, check_vma=False)
```

```python
import functools

import jax
import jax.numpy as jnp
from jax import lax
from jax.experimental import pallas as pl
from jax.experimental.pallas import tpu as pltpu
from jax.sharding import PartitionSpec as P

NZ, NX = 2, 4
PICK_CUTS = 4


def adam_update(weights, first, second, grad):
    first = 0.9 * first + 0.1 * grad
    second = 0.95 * second + 0.05 * grad * grad
    update = first / (jnp.sqrt(second) + 1e-08) + 0.1 * weights
    return (weights - 0.001 * update, first, second, update)


def outer_nesterov(outer, momentum, delta):
    momentum_new = 0.9 * momentum + delta
    return (outer - 0.7 * (0.9 * momentum_new + delta), momentum_new)


def shift(value, dz, dx):
    pairs = [
        (z * NX + x, (z + dz) % NZ * NX + (x + dx) % NX) for z in range(NZ) for x in range(NX)
    ]
    return lax.ppermute(value, "fsdp", pairs)


def f32(value):
    return value.astype(jnp.float32)


def bf16(value):
    return value.astype(jnp.bfloat16)


def dot(a, b):
    return jnp.dot(a, b, preferred_element_type=jnp.float32)


def tie(*values):
    return lax.optimization_barrier(values)


def dot_t(a, b):
    return lax.dot_general(a, b, (((0,), (0,)), ((), ())), preferred_element_type=jnp.float32)


def pick_kernel(dx, x_ref, o_ref, held_ref, in_sems, out_sems):
    rows = o_ref.shape[1] // NZ
    tile = o_ref.shape[0] // PICK_CUTS
    me = lax.axis_index("fsdp")
    loads, stores = [], []
    for dz in range(NZ):
        owner = lax.rem(me // NX + dz, NZ) * NX + lax.rem(lax.rem(me, NX) + dx, NX)
        start = pl.multiple_of(owner * rows, rows)
        for cut in range(PICK_CUTS):
            span, place = pl.ds(cut * tile, tile), pl.ds(dz * rows, rows)
            loads.append(
                pltpu.make_async_copy(
                    x_ref.at[span, pl.ds(start, rows)],
                    held_ref.at[span, place],
                    in_sems.at[dz, cut],
                )
            )
            stores.append(
                pltpu.make_async_copy(
                    held_ref.at[span, place], o_ref.at[span, place], out_sems.at[dz, cut]
                )
            )
    for load in loads:
        load.start()
    for load, store in zip(loads, stores):
        load.wait()
        store.start()
    for store in stores:
        store.wait()


def pick(inputs, dx, rows):
    tokens = inputs.shape[0]
    return pl.pallas_call(
        functools.partial(pick_kernel, dx),
        out_shape=jax.ShapeDtypeStruct((tokens, NZ * rows), inputs.dtype),
        in_specs=[pl.BlockSpec(memory_space=pl.ANY)],
        out_specs=pl.BlockSpec(memory_space=pl.ANY),
        scratch_shapes=[
            pltpu.VMEM((tokens, NZ * rows), inputs.dtype),
            pltpu.SemaphoreType.DMA((NZ, PICK_CUTS)),
            pltpu.SemaphoreType.DMA((NZ, PICK_CUTS)),
        ],
        cost_estimate=pl.CostEstimate(
            flops=0, bytes_accessed=4 * tokens * NZ * rows, transcendentals=0
        ),
    )(inputs)


def send_parts(parts):
    return {dx: shift(parts[dx], 0, -dx) for dx in parts}


def add_parts(outputs, arrived):
    for dx in (1, 3, 2):
        outputs = outputs + f32(arrived[dx])
    return outputs


def shards(
    tokens, targets, block_master, block_first, block_second, frag_outer, frag_inner, frag_momentum
):
    inputs = tokens[0]
    groups = lax.axis_size("fsdp")
    replicas = lax.axis_size("rep")
    tok_local, features = inputs.shape
    tok_all = tok_local * groups
    rows, width = block_master.shape[1:]
    half = width // 2
    span_a, span_b = slice(0, half), slice(half, width)

    blocks = [None] * NX
    for dx in (2, 1, 3):
        picked = pick(inputs, dx, rows)
        blocks[dx] = shift(picked, 0, dx)
    master, picked = tie(block_master[0], picked)
    sent = bf16(master)
    blocks[0] = pick(inputs, 0, rows)
    both = jnp.concatenate([sent, shift(sent, 1, 0)], axis=0)

    frag_rows = frag_inner.shape[1] // replicas
    pieces = lax.all_to_all(
        frag_inner[0].reshape(replicas, frag_rows, -1), "rep", 0, 0
    )
    blocks[1], blocks[2], blocks[3], pieces = tie(blocks[1], blocks[2], blocks[3], pieces)
    inner_sum = lax.all_gather(jnp.sum(f32(pieces), axis=0), "rep", axis=0, tiled=True)

    teacher = f32(targets[0])
    (own,) = tie(dot(blocks[0], both))
    part = {dx: dot(blocks[dx], both) for dx in (1, 2, 3)}
    arrived_a = send_parts({dx: bf16(part[dx][:, span_a]) for dx in (1, 2, 3)})
    resid_a = bf16(add_parts(own[:, span_a], arrived_a) - teacher[:, span_a])
    part_b = {dx: bf16(part[dx][:, span_b]) for dx in (1, 2, 3)}
    part_b[1], part_b[2], part_b[3], resid_a = tie(part_b[1], part_b[2], part_b[3], resid_a)
    arrived_b = send_parts(part_b)
    resid_b = bf16(add_parts(own[:, span_b], arrived_b) - teacher[:, span_b])
    (held,) = tie(jnp.concatenate(blocks, axis=0))

    def state(span):
        return [x[0, :, span] for x in (block_master, block_first, block_second)]

    def gather(resid):
        return [resid] + [shift(resid, 0, dx) for dx in range(1, NX)]

    def near(row):
        return dot_t(held[:, :rows], row)

    def away(row):
        return bf16(dot_t(held[:, rows:], row))

    def step_one(resid_a, resid_b):
        row_a = jnp.concatenate(gather(resid_a), axis=0)
        row_b = jnp.concatenate(gather(resid_b), axis=0)
        away_a = away(row_a)
        got_a = shift(away_a, 1, 0)
        row_b, away_a = tie(row_b, away_a)
        away_b = away(row_b)
        got_b = shift(away_b, 1, 0)
        row_a, row_b, away_b = tie(row_a, row_b, away_b)
        return near(row_a), near(row_b), got_a, got_b

    own_a, own_b, got_a, got_b = step_one(resid_a, resid_b)
    grad_a = (own_a + f32(got_a)) / tok_all
    *state_a, update_a = adam_update(*state(span_a), grad_a)
    sent_a = bf16(state_a[0])
    sent_a, own_b = tie(sent_a, own_b)
    other_a = shift(sent_a, 1, 0)
    grad_b = (own_b + f32(got_b)) / tok_all
    *state_b, update_b = adam_update(*state(span_b), grad_b)
    sent_b = bf16(state_b[0])
    other_b = shift(sent_b, 1, 0)
    sent_a, sent_b = tie(sent_a, sent_b)

    both_a = jnp.concatenate([sent_a, other_a], axis=0)
    part_a = dot(held, both_a).reshape(NX, tok_local, half)
    arrived_a = send_parts({dx: bf16(part_a[dx]) for dx in (2, 1, 3)})
    both_b = jnp.concatenate([sent_b, other_b], axis=0)
    part_b = dot(held, both_b).reshape(NX, tok_local, half)
    arrived_b = send_parts({dx: bf16(part_b[dx]) for dx in (2, 1, 3)})
    resid_a = bf16(add_parts(part_a[0], arrived_a) - teacher[:, span_a])
    arrived_b[1], resid_a = tie(arrived_b[1], resid_a)
    resid_b = bf16(add_parts(part_b[0], arrived_b) - teacher[:, span_b])
    delta = frag_outer - inner_sum / replicas
    frag_params, momentum_out = outer_nesterov(frag_outer, frag_momentum, delta)
    own_a, own_b, got_a, got_b = step_one(resid_a, resid_b)
    own_a, own_b, frag_params, momentum_out = tie(own_a, own_b, frag_params, momentum_out)
    grad_a = (own_a + f32(got_a)) / tok_all
    total_a = update_a + adam_update(*state_a, grad_a)[3]
    total_a, own_b = tie(total_a, own_b)
    grad_b = (own_b + f32(got_b)) / tok_all
    total_b = update_b + adam_update(*state_b, grad_b)[3]
    block_shift = jnp.concatenate([total_a, total_b], axis=1)
    return (block_shift[None], frag_params, momentum_out)


def solution(mesh):
    in_specs = (
        P("rep", "fsdp", None),
        P("rep", "fsdp", None),
        P("rep", "fsdp", None),
        P("rep", "fsdp", None),
        P("rep", "fsdp", None),
        P("fsdp", None),
        P("rep", "fsdp", None),
        P("fsdp", None),
    )
    out_specs = (P("rep", "fsdp", None), P("fsdp", None), P("fsdp", None))
    return jax.shard_map(shards, mesh=mesh, in_specs=in_specs, out_specs=out_specs, check_vma=False)
```

```python
import functools

import jax
import jax.numpy as jnp
from jax import lax
from jax.experimental import pallas as pl
from jax.experimental.pallas import tpu as pltpu
from jax.sharding import PartitionSpec as P

NZ, NX = 2, 4
PICK_CUTS = 4


def adam_update(weights, first, second, grad):
    first = 0.9 * first + 0.1 * grad
    second = 0.95 * second + 0.05 * grad * grad
    update = first / (jnp.sqrt(second) + 1e-08) + 0.1 * weights
    return (weights - 0.001 * update, first, second, update)


def outer_nesterov(outer, momentum, delta):
    momentum_new = 0.9 * momentum + delta
    return (outer - 0.7 * (0.9 * momentum_new + delta), momentum_new)


def shift(value, dz, dx):
    pairs = [
        (z * NX + x, (z + dz) % NZ * NX + (x + dx) % NX) for z in range(NZ) for x in range(NX)
    ]
    return lax.ppermute(value, "fsdp", pairs)


def f32(value):
    return value.astype(jnp.float32)


def bf16(value):
    return value.astype(jnp.bfloat16)


def dot(a, b):
    return jnp.dot(a, b, preferred_element_type=jnp.float32)


def tie(*values):
    return lax.optimization_barrier(values)


def dot_t(a, b):
    return lax.dot_general(a, b, (((0,), (0,)), ((), ())), preferred_element_type=jnp.float32)


def pick_kernel(dx, x_ref, o_ref, held_ref, in_sems, out_sems):
    rows = o_ref.shape[1] // NZ
    tile = o_ref.shape[0] // PICK_CUTS
    me = lax.axis_index("fsdp")
    loads, stores = [], []
    for dz in range(NZ):
        owner = lax.rem(me // NX + dz, NZ) * NX + lax.rem(lax.rem(me, NX) + dx, NX)
        start = pl.multiple_of(owner * rows, rows)
        for cut in range(PICK_CUTS):
            span, place = pl.ds(cut * tile, tile), pl.ds(dz * rows, rows)
            loads.append(
                pltpu.make_async_copy(
                    x_ref.at[span, pl.ds(start, rows)],
                    held_ref.at[span, place],
                    in_sems.at[dz, cut],
                )
            )
            stores.append(
                pltpu.make_async_copy(
                    held_ref.at[span, place], o_ref.at[span, place], out_sems.at[dz, cut]
                )
            )
    for load in loads:
        load.start()
    for load, store in zip(loads, stores):
        load.wait()
        store.start()
    for store in stores:
        store.wait()


def pick(inputs, dx, rows):
    tokens = inputs.shape[0]
    return pl.pallas_call(
        functools.partial(pick_kernel, dx),
        out_shape=jax.ShapeDtypeStruct((tokens, NZ * rows), inputs.dtype),
        in_specs=[pl.BlockSpec(memory_space=pl.ANY)],
        out_specs=pl.BlockSpec(memory_space=pl.ANY),
        scratch_shapes=[
            pltpu.VMEM((tokens, NZ * rows), inputs.dtype),
            pltpu.SemaphoreType.DMA((NZ, PICK_CUTS)),
            pltpu.SemaphoreType.DMA((NZ, PICK_CUTS)),
        ],
        cost_estimate=pl.CostEstimate(
            flops=0, bytes_accessed=4 * tokens * NZ * rows, transcendentals=0
        ),
    )(inputs)


def send_parts(parts):
    return {dx: shift(parts[dx], 0, -dx) for dx in parts}


def add_parts(outputs, arrived):
    for dx in (1, 3, 2):
        outputs = outputs + f32(arrived[dx])
    return outputs


def shards(
    tokens, targets, block_master, block_first, block_second, frag_outer, frag_inner, frag_momentum
):
    inputs = tokens[0]
    groups = lax.axis_size("fsdp")
    replicas = lax.axis_size("rep")
    tok_local, features = inputs.shape
    tok_all = tok_local * groups
    rows, width = block_master.shape[1:]
    half = width // 2
    span_a, span_b = slice(0, half), slice(half, width)

    blocks = [None] * NX
    for dx in (2, 1, 3):
        picked = pick(inputs, dx, rows)
        blocks[dx] = shift(picked, 0, dx)
    master, picked = tie(block_master[0], picked)
    sent = bf16(master)
    blocks[0] = pick(inputs, 0, rows)
    both = jnp.concatenate([sent, shift(sent, 1, 0)], axis=0)

    mates = replicas // 2
    rep_groups = [list(range(mates)), list(range(mates, replicas))]
    across = [(r, (r + mates) % replicas) for r in range(replicas)]
    frag_rows = frag_inner.shape[1] // mates
    pieces = lax.all_to_all(
        frag_inner[0].reshape(mates, frag_rows, -1), "rep", 0, 0, axis_index_groups=rep_groups
    )
    blocks[1], blocks[2], blocks[3], pieces = tie(blocks[1], blocks[2], blocks[3], pieces)
    piece_sum = jnp.sum(f32(pieces), axis=0)
    piece_sum = piece_sum + lax.ppermute(piece_sum, "rep", across)

    teacher = f32(targets[0])
    part = {dx: bf16(dot(blocks[dx], both)) for dx in (1, 2, 3)}
    arrived = send_parts(part)
    blocks[0], part[1], part[2], part[3] = tie(blocks[0], part[1], part[2], part[3])
    own = dot(blocks[0], both)
    own, *blocks = tie(own, *blocks)
    outputs = add_parts(own, arrived)
    resid_a = bf16(outputs[:, span_a] - teacher[:, span_a])
    resid_b = bf16(outputs[:, span_b] - teacher[:, span_b])
    (held,) = tie(jnp.concatenate(blocks, axis=0))

    def state(span):
        return [x[0, :, span] for x in (block_master, block_first, block_second)]

    def gather(resid):
        return [resid] + [shift(resid, 0, dx) for dx in range(1, NX)]

    def near(row):
        return dot_t(held[:, :rows], row)

    def away(row):
        return bf16(dot_t(held[:, rows:], row))

    def step_one(resid_a, resid_b):
        row_a = jnp.concatenate(gather(resid_a), axis=0)
        row_b = jnp.concatenate(gather(resid_b), axis=0)
        away_a = away(row_a)
        got_a = shift(away_a, 1, 0)
        row_b, away_a = tie(row_b, away_a)
        away_b = away(row_b)
        got_b = shift(away_b, 1, 0)
        row_a, row_b, away_b = tie(row_a, row_b, away_b)
        return near(row_a), near(row_b), got_a, got_b

    own_a, own_b, got_a, got_b = step_one(resid_a, resid_b)
    grad_a = (own_a + f32(got_a)) / tok_all
    *state_a, update_a = adam_update(*state(span_a), grad_a)
    sent_a = bf16(state_a[0])
    sent_a, own_b = tie(sent_a, own_b)
    other_a = shift(sent_a, 1, 0)
    grad_b = (own_b + f32(got_b)) / tok_all
    *state_b, update_b = adam_update(*state(span_b), grad_b)
    sent_b = bf16(state_b[0])
    other_b = shift(sent_b, 1, 0)
    sent_a, sent_b, piece_sum = tie(sent_a, sent_b, piece_sum)
    inner_sum = lax.all_to_all(
        jnp.broadcast_to(piece_sum[None], (mates, *piece_sum.shape)),
        "rep",
        0,
        0,
        axis_index_groups=rep_groups,
    ).reshape(frag_outer.shape)
    delta = frag_outer - inner_sum / replicas
    frag_params, momentum_out = outer_nesterov(frag_outer, frag_momentum, delta)

    both_a = jnp.concatenate([sent_a, other_a], axis=0)
    part_a = bf16(dot(held, both_a)).reshape(NX, tok_local, half)
    arrived_a = send_parts({dx: part_a[dx] for dx in (2, 1, 3)})
    both_b = jnp.concatenate([sent_b, other_b], axis=0)
    part_b = bf16(dot(held, both_b)).reshape(NX, tok_local, half)
    arrived_b = send_parts({dx: part_b[dx] for dx in (2, 1, 3)})
    resid_a = bf16(add_parts(f32(part_a[0]), arrived_a) - teacher[:, span_a])
    row_a = jnp.concatenate(gather(resid_a), axis=0)
    away_a = away(row_a)
    got_a = shift(away_a, 1, 0)
    own_b, away_a = tie(part_b[0], away_a)
    resid_b = bf16(add_parts(f32(own_b), arrived_b) - teacher[:, span_b])
    row_b = jnp.concatenate(gather(resid_b), axis=0)
    away_b = away(row_b)
    got_b = shift(away_b, 1, 0)
    row_a, row_b, away_b = tie(row_a, row_b, away_b)
    own_a, own_b = near(row_a), near(row_b)
    own_a, own_b, frag_params, momentum_out = tie(own_a, own_b, frag_params, momentum_out)
    grad_a = (own_a + f32(got_a)) / tok_all
    total_a = update_a + adam_update(*state_a, grad_a)[3]
    total_a, own_b = tie(total_a, own_b)
    grad_b = (own_b + f32(got_b)) / tok_all
    total_b = update_b + adam_update(*state_b, grad_b)[3]
    block_shift = jnp.concatenate([total_a, total_b], axis=1)
    return (block_shift[None], frag_params, momentum_out)


def solution(mesh):
    in_specs = (
        P("rep", "fsdp", None),
        P("rep", "fsdp", None),
        P("rep", "fsdp", None),
        P("rep", "fsdp", None),
        P("rep", "fsdp", None),
        P("fsdp", None),
        P("rep", "fsdp", None),
        P("fsdp", None),
    )
    out_specs = (P("rep", "fsdp", None), P("fsdp", None), P("fsdp", None))
    return jax.shard_map(shards, mesh=mesh, in_specs=in_specs, out_specs=out_specs, check_vma=False)
```

```python
import functools

import jax
import jax.numpy as jnp
from jax import lax
from jax.experimental import pallas as pl
from jax.experimental.pallas import tpu as pltpu
from jax.sharding import PartitionSpec as P

NZ, NX = 2, 4
PICK_CUTS = 4


def adam_update(weights, first, second, grad):
    first = 0.9 * first + 0.1 * grad
    second = 0.95 * second + 0.05 * grad * grad
    update = first / (jnp.sqrt(second) + 1e-08) + 0.1 * weights
    return (weights - 0.001 * update, first, second, update)


def outer_nesterov(outer, momentum, delta):
    momentum_new = 0.9 * momentum + delta
    return (outer - 0.7 * (0.9 * momentum_new + delta), momentum_new)


def shift(value, dz, dx):
    pairs = [
        (z * NX + x, (z + dz) % NZ * NX + (x + dx) % NX) for z in range(NZ) for x in range(NX)
    ]
    return lax.ppermute(value, "fsdp", pairs)


def f32(value):
    return value.astype(jnp.float32)


def bf16(value):
    return value.astype(jnp.bfloat16)


def dot(a, b):
    return jnp.dot(a, b, preferred_element_type=jnp.float32)


def tie(*values):
    return lax.optimization_barrier(values)


def dot_t(a, b):
    return lax.dot_general(a, b, (((0,), (0,)), ((), ())), preferred_element_type=jnp.float32)


def pick_kernel(dx, x_ref, o_ref, held_ref, in_sems, out_sems):
    rows = o_ref.shape[1] // NZ
    tile = o_ref.shape[0] // PICK_CUTS
    me = lax.axis_index("fsdp")
    loads, stores = [], []
    for dz in range(NZ):
        owner = lax.rem(me // NX + dz, NZ) * NX + lax.rem(lax.rem(me, NX) + dx, NX)
        start = pl.multiple_of(owner * rows, rows)
        for cut in range(PICK_CUTS):
            span, place = pl.ds(cut * tile, tile), pl.ds(dz * rows, rows)
            loads.append(
                pltpu.make_async_copy(
                    x_ref.at[span, pl.ds(start, rows)],
                    held_ref.at[span, place],
                    in_sems.at[dz, cut],
                )
            )
            stores.append(
                pltpu.make_async_copy(
                    held_ref.at[span, place], o_ref.at[span, place], out_sems.at[dz, cut]
                )
            )
    for load in loads:
        load.start()
    for load, store in zip(loads, stores):
        load.wait()
        store.start()
    for store in stores:
        store.wait()


def pick(inputs, dx, rows):
    tokens = inputs.shape[0]
    return pl.pallas_call(
        functools.partial(pick_kernel, dx),
        out_shape=jax.ShapeDtypeStruct((tokens, NZ * rows), inputs.dtype),
        in_specs=[pl.BlockSpec(memory_space=pl.ANY)],
        out_specs=pl.BlockSpec(memory_space=pl.ANY),
        scratch_shapes=[
            pltpu.VMEM((tokens, NZ * rows), inputs.dtype),
            pltpu.SemaphoreType.DMA((NZ, PICK_CUTS)),
            pltpu.SemaphoreType.DMA((NZ, PICK_CUTS)),
        ],
        cost_estimate=pl.CostEstimate(
            flops=0, bytes_accessed=4 * tokens * NZ * rows, transcendentals=0
        ),
    )(inputs)


def send_parts(parts):
    return {dx: shift(parts[dx], 0, -dx) for dx in parts}


def add_parts(outputs, arrived):
    for dx in (1, 3, 2):
        outputs = outputs + f32(arrived[dx])
    return outputs


def shards(
    tokens, targets, block_master, block_first, block_second, frag_outer, frag_inner, frag_momentum
):
    inputs = tokens[0]
    groups = lax.axis_size("fsdp")
    replicas = lax.axis_size("rep")
    tok_local, features = inputs.shape
    tok_all = tok_local * groups
    rows, width = block_master.shape[1:]
    half = width // 2
    span_a, span_b = slice(0, half), slice(half, width)

    blocks = [None] * NX
    for dx in (2, 1, 3):
        picked = pick(inputs, dx, rows)
        blocks[dx] = shift(picked, 0, dx)
    master, picked = tie(block_master[0], picked)
    sent = bf16(master)
    blocks[0] = pick(inputs, 0, rows)
    both = jnp.concatenate([sent, shift(sent, 1, 0)], axis=0)

    mates = replicas // 2
    rep_groups = [list(range(mates)), list(range(mates, replicas))]
    across = [(r, (r + mates) % replicas) for r in range(replicas)]
    frag_rows = frag_inner.shape[1] // mates
    pieces = lax.all_to_all(
        frag_inner[0].reshape(mates, frag_rows, -1), "rep", 0, 0, axis_index_groups=rep_groups
    )
    blocks[1], blocks[3], pieces = tie(blocks[1], blocks[3], pieces)
    piece_sum = jnp.sum(f32(pieces), axis=0)
    piece_sum = (piece_sum + lax.ppermute(piece_sum, "rep", across)) / replicas

    teacher = f32(targets[0])
    part = {dx: bf16(dot(blocks[dx], both)) for dx in (1, 2, 3)}
    arrived = send_parts(part)
    blocks[0], part[1], part[2], part[3] = tie(blocks[0], part[1], part[2], part[3])
    own = dot(blocks[0], both)
    own, *blocks = tie(own, *blocks)
    outputs = add_parts(own, arrived)
    resid_a = bf16(outputs[:, span_a] - teacher[:, span_a])
    resid_b = bf16(outputs[:, span_b] - teacher[:, span_b])
    (held,) = tie(jnp.concatenate(blocks, axis=0))

    def state(span):
        return [x[0, :, span] for x in (block_master, block_first, block_second)]

    def gather(resid):
        return [resid] + [shift(resid, 0, dx) for dx in range(1, NX)]

    def near(row):
        return dot_t(held[:, :rows], row)

    def away(row):
        return bf16(dot_t(held[:, rows:], row))

    def step_one(resid_a, resid_b):
        row_a = jnp.concatenate(gather(resid_a), axis=0)
        row_b = jnp.concatenate(gather(resid_b), axis=0)
        away_a = away(row_a)
        got_a = shift(away_a, 1, 0)
        row_b, away_a = tie(row_b, away_a)
        away_b = away(row_b)
        got_b = shift(away_b, 1, 0)
        row_a, row_b, away_b = tie(row_a, row_b, away_b)
        return near(row_a), near(row_b), got_a, got_b

    own_a, own_b, got_a, got_b = step_one(resid_a, resid_b)
    grad_a = (own_a + f32(got_a)) / tok_all
    *state_a, update_a = adam_update(*state(span_a), grad_a)
    sent_a = bf16(state_a[0])
    sent_a, own_b = tie(sent_a, own_b)
    other_a = shift(sent_a, 1, 0)
    grad_b = (own_b + f32(got_b)) / tok_all
    *state_b, update_b = adam_update(*state(span_b), grad_b)
    sent_b = bf16(state_b[0])
    other_b = shift(sent_b, 1, 0)
    sent_a, sent_b, piece_sum = tie(sent_a, sent_b, piece_sum)
    inner_sum = lax.all_to_all(
        jnp.broadcast_to(piece_sum[None], (mates, *piece_sum.shape)),
        "rep",
        0,
        0,
        axis_index_groups=rep_groups,
    ).reshape(frag_outer.shape)
    delta = frag_outer - inner_sum
    frag_params, momentum_out = outer_nesterov(frag_outer, frag_momentum, delta)

    both_a = jnp.concatenate([sent_a, other_a], axis=0)
    part_a = bf16(dot(held, both_a)).reshape(NX, tok_local, half)
    arrived_a = send_parts({dx: part_a[dx] for dx in (2, 1, 3)})
    both_b = jnp.concatenate([sent_b, other_b], axis=0)
    part_b = bf16(dot(held, both_b)).reshape(NX, tok_local, half)
    arrived_b = send_parts({dx: part_b[dx] for dx in (2, 1, 3)})
    resid_a = bf16(add_parts(f32(part_a[0]), arrived_a) - teacher[:, span_a])
    row_a = jnp.concatenate(gather(resid_a), axis=0)
    away_a = away(row_a)
    got_a = shift(away_a, 1, 0)
    own_b, away_a = tie(part_b[0], away_a)
    resid_b = bf16(add_parts(f32(own_b), arrived_b) - teacher[:, span_b])
    row_b = jnp.concatenate(gather(resid_b), axis=0)
    away_b = away(row_b)
    got_b = shift(away_b, 1, 0)
    row_a, row_b, away_b = tie(row_a, row_b, away_b)
    own_a, own_b = near(row_a), near(row_b)
    own_a, own_b, frag_params, momentum_out = tie(own_a, own_b, frag_params, momentum_out)
    grad_a = (own_a + f32(got_a)) / tok_all
    total_a = update_a + adam_update(*state_a, grad_a)[3]
    total_a, own_b = tie(total_a, own_b)
    grad_b = (own_b + f32(got_b)) / tok_all
    total_b = update_b + adam_update(*state_b, grad_b)[3]
    block_shift = jnp.concatenate([total_a, total_b], axis=1)
    return (block_shift[None], frag_params, momentum_out)


def solution(mesh):
    in_specs = (
        P("rep", "fsdp", None),
        P("rep", "fsdp", None),
        P("rep", "fsdp", None),
        P("rep", "fsdp", None),
        P("rep", "fsdp", None),
        P("fsdp", None),
        P("rep", "fsdp", None),
        P("fsdp", None),
    )
    out_specs = (P("rep", "fsdp", None), P("fsdp", None), P("fsdp", None))
    return jax.shard_map(shards, mesh=mesh, in_specs=in_specs, out_specs=out_specs, check_vma=False)
```

```python
import functools

import jax
import jax.numpy as jnp
from jax import lax
from jax.experimental import pallas as pl
from jax.experimental.pallas import tpu as pltpu
from jax.sharding import PartitionSpec as P

NZ, NX = 2, 4
PICK_CUTS = 4


def adam_update(weights, first, second, grad):
    first = 0.9 * first + 0.1 * grad
    second = 0.95 * second + 0.05 * grad * grad
    update = first / (jnp.sqrt(second) + 1e-08) + 0.1 * weights
    return (weights - 0.001 * update, first, second, update)


def outer_nesterov(outer, momentum, delta):
    momentum_new = 0.9 * momentum + delta
    return (outer - 0.7 * (0.9 * momentum_new + delta), momentum_new)


def shift(value, dz, dx):
    pairs = [
        (z * NX + x, (z + dz) % NZ * NX + (x + dx) % NX) for z in range(NZ) for x in range(NX)
    ]
    return lax.ppermute(value, "fsdp", pairs)


def f32(value):
    return value.astype(jnp.float32)


def bf16(value):
    return value.astype(jnp.bfloat16)


def dot(a, b):
    return jnp.dot(a, b, preferred_element_type=jnp.float32)


def tie(*values):
    return lax.optimization_barrier(values)


def dot_t(a, b):
    return lax.dot_general(a, b, (((0,), (0,)), ((), ())), preferred_element_type=jnp.float32)


def pick_kernel(dx, x_ref, o_ref, held_ref, in_sems, out_sems):
    rows = o_ref.shape[1] // NZ
    tile = o_ref.shape[0] // PICK_CUTS
    me = lax.axis_index("fsdp")
    loads, stores = [], []
    for dz in range(NZ):
        owner = lax.rem(me // NX + dz, NZ) * NX + lax.rem(lax.rem(me, NX) + dx, NX)
        start = pl.multiple_of(owner * rows, rows)
        for cut in range(PICK_CUTS):
            span, place = pl.ds(cut * tile, tile), pl.ds(dz * rows, rows)
            loads.append(
                pltpu.make_async_copy(
                    x_ref.at[span, pl.ds(start, rows)],
                    held_ref.at[span, place],
                    in_sems.at[dz, cut],
                )
            )
            stores.append(
                pltpu.make_async_copy(
                    held_ref.at[span, place], o_ref.at[span, place], out_sems.at[dz, cut]
                )
            )
    for load in loads:
        load.start()
    for load, store in zip(loads, stores):
        load.wait()
        store.start()
    for store in stores:
        store.wait()


def pick(inputs, dx, rows):
    tokens = inputs.shape[0]
    return pl.pallas_call(
        functools.partial(pick_kernel, dx),
        out_shape=jax.ShapeDtypeStruct((tokens, NZ * rows), inputs.dtype),
        in_specs=[pl.BlockSpec(memory_space=pl.ANY)],
        out_specs=pl.BlockSpec(memory_space=pl.ANY),
        scratch_shapes=[
            pltpu.VMEM((tokens, NZ * rows), inputs.dtype),
            pltpu.SemaphoreType.DMA((NZ, PICK_CUTS)),
            pltpu.SemaphoreType.DMA((NZ, PICK_CUTS)),
        ],
        cost_estimate=pl.CostEstimate(
            flops=0, bytes_accessed=4 * tokens * NZ * rows, transcendentals=0
        ),
    )(inputs)


def send_parts(parts):
    return {dx: shift(parts[dx], 0, -dx) for dx in parts}


def add_parts(outputs, arrived):
    for dx in (1, 3, 2):
        outputs = outputs + f32(arrived[dx])
    return outputs


def shards(
    tokens, targets, block_master, block_first, block_second, frag_outer, frag_inner, frag_momentum
):
    inputs = tokens[0]
    groups = lax.axis_size("fsdp")
    replicas = lax.axis_size("rep")
    tok_local, features = inputs.shape
    tok_all = tok_local * groups
    rows, width = block_master.shape[1:]
    half = width // 2
    span_a, span_b = slice(0, half), slice(half, width)

    blocks = [None] * NX
    for dx in (2, 1, 3):
        picked = pick(inputs, dx, rows)
        blocks[dx] = shift(picked, 0, dx)
    master, picked = tie(block_master[0], picked)
    sent = bf16(master)
    blocks[0] = pick(inputs, 0, rows)
    both = jnp.concatenate([sent, shift(sent, 1, 0)], axis=0)

    mates = replicas // 2
    rep_groups = [list(range(mates)), list(range(mates, replicas))]
    across = [(r, (r + mates) % replicas) for r in range(replicas)]
    frag_rows = frag_inner.shape[1] // mates
    pieces = lax.all_to_all(
        frag_inner[0].reshape(mates, frag_rows, -1), "rep", 0, 0, axis_index_groups=rep_groups
    )
    blocks[1], blocks[3], pieces = tie(blocks[1], blocks[3], pieces)
    piece_sum = jnp.sum(f32(pieces), axis=0)
    piece_sum = (piece_sum + lax.ppermute(piece_sum, "rep", across)) / replicas

    teacher = f32(targets[0])
    part = {dx: bf16(dot(blocks[dx], both)) for dx in (1, 2, 3)}
    arrived = send_parts(part)
    own = dot(blocks[0], both)
    own, *blocks = tie(own, *blocks)
    outputs = add_parts(own, arrived)
    resid_a = bf16(outputs[:, span_a] - teacher[:, span_a])
    resid_b = bf16(outputs[:, span_b] - teacher[:, span_b])
    (held,) = tie(jnp.concatenate(blocks, axis=0))

    def state(span):
        return [x[0, :, span] for x in (block_master, block_first, block_second)]

    def gather(resid):
        return [resid] + [shift(resid, 0, dx) for dx in range(1, NX)]

    def near(row):
        return dot_t(held[:, :rows], row)

    def away(row):
        return bf16(dot_t(held[:, rows:], row))

    def step_one(resid_a, resid_b):
        row_a = jnp.concatenate(gather(resid_a), axis=0)
        row_b = jnp.concatenate(gather(resid_b), axis=0)
        away_a = away(row_a)
        got_a = shift(away_a, 1, 0)
        row_b, away_a = tie(row_b, away_a)
        away_b = away(row_b)
        got_b = shift(away_b, 1, 0)
        row_a, row_b, away_b = tie(row_a, row_b, away_b)
        return near(row_a), near(row_b), got_a, got_b

    own_a, own_b, got_a, got_b = step_one(resid_a, resid_b)
    grad_a = (own_a + f32(got_a)) / tok_all
    *state_a, update_a = adam_update(*state(span_a), grad_a)
    sent_a = bf16(state_a[0])
    sent_a, own_b = tie(sent_a, own_b)
    other_a = shift(sent_a, 1, 0)
    grad_b = (own_b + f32(got_b)) / tok_all
    *state_b, update_b = adam_update(*state(span_b), grad_b)
    sent_b = bf16(state_b[0])
    other_b = shift(sent_b, 1, 0)
    sent_a, sent_b, piece_sum = tie(sent_a, sent_b, piece_sum)
    inner_sum = lax.all_to_all(
        jnp.broadcast_to(piece_sum[None], (mates, *piece_sum.shape)),
        "rep",
        0,
        0,
        axis_index_groups=rep_groups,
    ).reshape(frag_outer.shape)
    delta = frag_outer - inner_sum
    frag_params, momentum_out = outer_nesterov(frag_outer, frag_momentum, delta)

    both_a = jnp.concatenate([sent_a, other_a], axis=0)
    part_a = bf16(dot(held, both_a)).reshape(NX, tok_local, half)
    arrived_a = send_parts({dx: part_a[dx] for dx in (2, 1, 3)})
    both_b = jnp.concatenate([sent_b, other_b], axis=0)
    part_b = bf16(dot(held, both_b)).reshape(NX, tok_local, half)
    arrived_b = send_parts({dx: part_b[dx] for dx in (2, 1, 3)})
    resid_a = bf16(add_parts(f32(part_a[0]), arrived_a) - teacher[:, span_a])
    row_a = jnp.concatenate(gather(resid_a), axis=0)
    away_a = away(row_a)
    got_a = shift(away_a, 1, 0)
    own_b, away_a = tie(part_b[0], away_a)
    resid_b = bf16(add_parts(f32(own_b), arrived_b) - teacher[:, span_b])
    row_b = jnp.concatenate(gather(resid_b), axis=0)
    away_b = away(row_b)
    got_b = shift(away_b, 1, 0)
    row_a, row_b, away_b = tie(row_a, row_b, away_b)
    own_a, own_b = near(row_a), near(row_b)
    grad_a = (own_a + f32(got_a)) / tok_all
    total_a = update_a + adam_update(*state_a, grad_a)[3]
    total_a, own_b, frag_params, momentum_out = tie(total_a, own_b, frag_params, momentum_out)
    grad_b = (own_b + f32(got_b)) / tok_all
    total_b = update_b + adam_update(*state_b, grad_b)[3]
    block_shift = jnp.concatenate([total_a, total_b], axis=1)
    return (block_shift[None], frag_params, momentum_out)


def solution(mesh):
    in_specs = (
        P("rep", "fsdp", None),
        P("rep", "fsdp", None),
        P("rep", "fsdp", None),
        P("rep", "fsdp", None),
        P("rep", "fsdp", None),
        P("fsdp", None),
        P("rep", "fsdp", None),
        P("fsdp", None),
    )
    out_specs = (P("rep", "fsdp", None), P("fsdp", None), P("fsdp", None))
    return jax.shard_map(shards, mesh=mesh, in_specs=in_specs, out_specs=out_specs, check_vma=False)
```

```python
import functools

import jax
import jax.numpy as jnp
from jax import lax
from jax.experimental import pallas as pl
from jax.experimental.pallas import tpu as pltpu
from jax.sharding import PartitionSpec as P

NZ, NX = 2, 4
PICK_CUTS = 4


def adam_update(weights, first, second, grad):
    first = 0.9 * first + 0.1 * grad
    second = 0.95 * second + 0.05 * grad * grad
    update = first / (jnp.sqrt(second) + 1e-08) + 0.1 * weights
    return (weights - 0.001 * update, first, second, update)


def outer_nesterov(outer, momentum, delta):
    momentum_new = 0.9 * momentum + delta
    return (outer - 0.7 * (0.9 * momentum_new + delta), momentum_new)


def shift(value, dz, dx):
    pairs = [
        (z * NX + x, (z + dz) % NZ * NX + (x + dx) % NX) for z in range(NZ) for x in range(NX)
    ]
    return lax.ppermute(value, "fsdp", pairs)


def f32(value):
    return value.astype(jnp.float32)


def bf16(value):
    return value.astype(jnp.bfloat16)


def dot(a, b):
    return jnp.dot(a, b, preferred_element_type=jnp.float32)


def tie(*values):
    return lax.optimization_barrier(values)


def dot_t(a, b):
    return lax.dot_general(a, b, (((0,), (0,)), ((), ())), preferred_element_type=jnp.float32)


def pick_kernel(dx, x_ref, o_ref, held_ref, in_sems, out_sems):
    rows = o_ref.shape[1] // NZ
    tile = o_ref.shape[0] // PICK_CUTS
    me = lax.axis_index("fsdp")
    loads, stores = [], []
    for dz in range(NZ):
        owner = lax.rem(me // NX + dz, NZ) * NX + lax.rem(lax.rem(me, NX) + dx, NX)
        start = pl.multiple_of(owner * rows, rows)
        for cut in range(PICK_CUTS):
            span, place = pl.ds(cut * tile, tile), pl.ds(dz * rows, rows)
            loads.append(
                pltpu.make_async_copy(
                    x_ref.at[span, pl.ds(start, rows)],
                    held_ref.at[span, place],
                    in_sems.at[dz, cut],
                )
            )
            stores.append(
                pltpu.make_async_copy(
                    held_ref.at[span, place], o_ref.at[span, place], out_sems.at[dz, cut]
                )
            )
    for load in loads:
        load.start()
    for load, store in zip(loads, stores):
        load.wait()
        store.start()
    for store in stores:
        store.wait()


def pick(inputs, dx, rows):
    tokens = inputs.shape[0]
    return pl.pallas_call(
        functools.partial(pick_kernel, dx),
        out_shape=jax.ShapeDtypeStruct((tokens, NZ * rows), inputs.dtype),
        in_specs=[pl.BlockSpec(memory_space=pl.ANY)],
        out_specs=pl.BlockSpec(memory_space=pl.ANY),
        scratch_shapes=[
            pltpu.VMEM((tokens, NZ * rows), inputs.dtype),
            pltpu.SemaphoreType.DMA((NZ, PICK_CUTS)),
            pltpu.SemaphoreType.DMA((NZ, PICK_CUTS)),
        ],
        cost_estimate=pl.CostEstimate(
            flops=0, bytes_accessed=4 * tokens * NZ * rows, transcendentals=0
        ),
    )(inputs)


def send_parts(parts):
    return {dx: shift(parts[dx], 0, -dx) for dx in parts}


def add_parts(outputs, arrived):
    for dx in (1, 3, 2):
        outputs = outputs + f32(arrived[dx])
    return outputs


def shards(
    tokens, targets, block_master, block_first, block_second, frag_outer, frag_inner, frag_momentum
):
    inputs = tokens[0]
    groups = lax.axis_size("fsdp")
    replicas = lax.axis_size("rep")
    tok_local, features = inputs.shape
    tok_all = tok_local * groups
    rows, width = block_master.shape[1:]
    half = width // 2
    span_a, span_b = slice(0, half), slice(half, width)

    blocks = [None] * NX
    for dx in (2, 1, 3):
        picked = pick(inputs, dx, rows)
        blocks[dx] = shift(picked, 0, dx)
    master, picked = tie(block_master[0], picked)
    sent = bf16(master)
    blocks[0] = pick(inputs, 0, rows)
    both = jnp.concatenate([sent, shift(sent, 1, 0)], axis=0)

    mates = replicas // 2
    rep_groups = [list(range(mates)), list(range(mates, replicas))]
    across = [(r, (r + mates) % replicas) for r in range(replicas)]
    frag_rows = frag_inner.shape[1] // mates
    pieces = lax.all_to_all(
        frag_inner[0].reshape(mates, frag_rows, -1), "rep", 0, 0, axis_index_groups=rep_groups
    )
    blocks[1], blocks[3], pieces = tie(blocks[1], blocks[3], pieces)
    piece_sum = jnp.sum(f32(pieces), axis=0)
    piece_sum = (piece_sum + lax.ppermute(piece_sum, "rep", across)) / replicas

    teacher = f32(targets[0])
    part = {dx: bf16(dot(blocks[dx], both)) for dx in (1, 2, 3)}
    arrived = send_parts(part)
    own = dot(blocks[0], both)
    own, *blocks = tie(own, *blocks)
    outputs = add_parts(own, arrived)
    resid_a = bf16(outputs[:, span_a] - teacher[:, span_a])
    resid_b = bf16(outputs[:, span_b] - teacher[:, span_b])
    (held,) = tie(jnp.concatenate(blocks, axis=0))

    def state(span):
        return [x[0, :, span] for x in (block_master, block_first, block_second)]

    def gather(resid):
        return [resid] + [shift(resid, 0, dx) for dx in range(1, NX)]

    def near(row):
        return dot_t(held[:, :rows], row)

    def away(row):
        return bf16(dot_t(held[:, rows:], row))

    def step_one(resid_a, resid_b):
        row_a = jnp.concatenate(gather(resid_a), axis=0)
        row_b = jnp.concatenate(gather(resid_b), axis=0)
        away_a = away(row_a)
        got_a = shift(away_a, 1, 0)
        row_b, away_a = tie(row_b, away_a)
        away_b = away(row_b)
        got_b = shift(away_b, 1, 0)
        row_a, row_b, away_b = tie(row_a, row_b, away_b)
        return near(row_a), near(row_b), got_a, got_b

    own_a, own_b, got_a, got_b = step_one(resid_a, resid_b)
    grad_a = (own_a + f32(got_a)) / tok_all
    *state_a, update_a = adam_update(*state(span_a), grad_a)
    sent_a = bf16(state_a[0])
    sent_a, own_b = tie(sent_a, own_b)
    other_a = shift(sent_a, 1, 0)
    grad_b = (own_b + f32(got_b)) / tok_all
    *state_b, update_b = adam_update(*state(span_b), grad_b)
    sent_b = bf16(state_b[0])
    other_b = shift(sent_b, 1, 0)
    sent_a, sent_b, piece_sum = tie(sent_a, sent_b, piece_sum)
    inner_sum = lax.all_to_all(
        jnp.broadcast_to(piece_sum[None], (mates, *piece_sum.shape)),
        "rep",
        0,
        0,
        axis_index_groups=rep_groups,
    ).reshape(frag_outer.shape)
    delta = frag_outer - inner_sum
    frag_params, momentum_out = outer_nesterov(frag_outer, frag_momentum, delta)

    both_a = jnp.concatenate([sent_a, other_a], axis=0)
    part_a = bf16(dot(held, both_a)).reshape(NX, tok_local, half)
    arrived_a = send_parts({dx: part_a[dx] for dx in (2, 1, 3)})
    both_b = jnp.concatenate([sent_b, other_b], axis=0)
    part_b = bf16(dot(held, both_b)).reshape(NX, tok_local, half)
    arrived_b = send_parts({dx: part_b[dx] for dx in (2, 1, 3)})
    resid_a = bf16(add_parts(f32(part_a[0]), arrived_a) - teacher[:, span_a])
    row_a = jnp.concatenate(gather(resid_a), axis=0)
    row_a, arrived_b[1], arrived_b[2], arrived_b[3] = tie(
        row_a, arrived_b[1], arrived_b[2], arrived_b[3]
    )
    away_a = away(row_a)
    got_a = shift(away_a, 1, 0)
    own_b, away_a = tie(part_b[0], away_a)
    resid_b = bf16(add_parts(f32(own_b), arrived_b) - teacher[:, span_b])
    row_b = jnp.concatenate(gather(resid_b), axis=0)
    away_b = away(row_b)
    got_b = shift(away_b, 1, 0)
    row_a, row_b, away_b = tie(row_a, row_b, away_b)
    own_a, own_b = near(row_a), near(row_b)
    grad_a = (own_a + f32(got_a)) / tok_all
    total_a = update_a + adam_update(*state_a, grad_a)[3]
    total_a, own_b, frag_params, momentum_out = tie(total_a, own_b, frag_params, momentum_out)
    grad_b = (own_b + f32(got_b)) / tok_all
    total_b = update_b + adam_update(*state_b, grad_b)[3]
    block_shift = jnp.concatenate([total_a, total_b], axis=1)
    return (block_shift[None], frag_params, momentum_out)


def solution(mesh):
    in_specs = (
        P("rep", "fsdp", None),
        P("rep", "fsdp", None),
        P("rep", "fsdp", None),
        P("rep", "fsdp", None),
        P("rep", "fsdp", None),
        P("fsdp", None),
        P("rep", "fsdp", None),
        P("fsdp", None),
    )
    out_specs = (P("rep", "fsdp", None), P("fsdp", None), P("fsdp", None))
    return jax.shard_map(shards, mesh=mesh, in_specs=in_specs, out_specs=out_specs, check_vma=False)
```
